512 devices in a mesh: lag: 8 (over x, core), par: 64 (over z, y).
Axes of the slice: x: 4, y: 4, z: 16, core: 2. Of those that a mesh axis runs over, the one named last changes fastest.
Arguments:
- probes: bfloat16 [32, 64, 8192], P('lag', None, 'par'), may hold values from -6 to 6
- lag_blocks: bfloat16 [32, 512, 8192], P('lag', None, 'par'), may hold values from -0.0234375 to 0.0234375
- sensor_weights: float32 [512], replicated, may hold values from 0.2 to 2
- sensor_mask: int32 [512], replicated, may hold values 0 or 1
Outputs:
- hessian_probes: float32 [32, 64, 8192], P('lag', None, 'par')
- sensor_grad: float32 [512], replicated
The draws below stay inside these ranges and needn't reach their ends.
All inputs are finite; a program needn't handle non-finite values.
Results may differ from the reference program's by a relative error of at most 0.0013.
Values may be sent and summed in bfloat16 or wider, within the bound.
A program may use at most 64 MiB of HBM per device.

```python
import math
import jax
import jax.numpy as jnp
from jax import lax

NS = 512
PROBES = 64
LAGS = 32
NPAR = 8192


def plant(drawn, rng, least, top_value):
    place = [jax.random.randint(jax.random.fold_in(rng, axis), (), 0, length) for axis, length in enumerate(drawn.shape)]
    widest = drawn.shape.index(max(drawn.shape))
    next_to = place[:widest] + [(place[widest] + 1) % drawn.shape[widest]] + place[widest + 1:]
    return drawn.at[tuple(place)].set(least).at[tuple(next_to)].set(top_value)


def level_of(rng, shape, split, low, top_value):
    factor_of, own = 1.0, jax.random.fold_in(rng, 6)
    for axis_at, parts in split:
        heights = jnp.exp(jax.random.uniform(jax.random.fold_in(own, axis_at), (parts,), jnp.float32, low / len(split), top_value / len(split)))
        factor_of = factor_of * jnp.repeat(heights, shape[axis_at] // parts).reshape([-1 if axis == axis_at else 1 for axis in range(len(shape))])
    return factor_of


def noise(rng, dims, spread, most, pieces=(), kind=jnp.bfloat16):
    entries = spread * jax.random.normal(rng, dims, jnp.float32)
    if pieces:
        entries = entries * level_of(rng, dims, pieces, -0.22, 0.18)
    return jnp.clip(entries, -most, most).astype(kind)


def setup_inputs(seed: int = 0) -> dict:
    splits = jax.random.split(jax.random.key(seed), 5)
    return {
        "probes": noise(splits[0], (LAGS, PROBES, NPAR), 1.0, 6.0, ((0, 8), (2, 64))),
        "lag_blocks": noise(splits[1], (LAGS, NS, NPAR), (4 * LAGS * NS) ** -0.5, 0.0234375, ((0, 8), (2, 64))),
        "sensor_weights": jnp.clip(jnp.exp(jax.random.uniform(splits[2], (NS,), jnp.float32, math.log(0.2), math.log(2.0))), 0.2, 2.0),
        "sensor_mask": plant((jax.random.randint(splits[3], (NS,), 0, 4) < 3).astype(jnp.int32), jax.random.fold_in(splits[3], 1), 0, 1),
    }


def reference(probes, lag_blocks, sensor_weights, sensor_mask):
    time_steps = probes.shape[0]
    flat_rows = time_steps * PROBES
    flat_probes = probes.reshape(flat_rows, NPAR)
    active = sensor_mask.astype(jnp.float32)
    lag_numbers = jnp.arange(LAGS, dtype=jnp.int32)

    def forward(running, inputs):
        lag_block, lag_index = inputs
        product = jnp.dot(flat_probes, lag_block.T, preferred_element_type=jnp.float32).reshape(time_steps, PROBES, NS)
        padded = jnp.concatenate([jnp.zeros_like(product), product], 0)
        shifted = lax.dynamic_slice_in_dim(padded, (time_steps - lag_index).astype(jnp.int32), time_steps, 0)
        return running + shifted, None

    observed, _ = lax.scan(forward, jnp.zeros((time_steps, PROBES, NS), jnp.float32), (lag_blocks, lag_numbers))
    weighted = (sensor_weights * active * observed).astype(jnp.bfloat16)
    padded_weighted = jnp.concatenate([weighted, jnp.zeros_like(weighted)], 0)

    def adjoint(running, inputs):
        lag_block, lag_index = inputs
        later = lax.dynamic_slice_in_dim(padded_weighted, lag_index.astype(jnp.int32), time_steps, 0)
        product = jnp.dot(later.reshape(flat_rows, NS), lag_block, preferred_element_type=jnp.float32)
        return running + product.reshape(time_steps, PROBES, NPAR), None

    misfit, _ = lax.scan(adjoint, jnp.zeros((time_steps, PROBES, NPAR), jnp.float32), (lag_blocks, lag_numbers))
    hessian_probes = misfit + probes.astype(jnp.float32)
    sensor_grad = active * jnp.sum(observed * observed, axis=(0, 1)) / (time_steps * PROBES)
    return hessian_probes, sensor_grad
```

```python
import functools

import jax
import jax.numpy as jnp
from jax import lax
from jax.experimental import pallas as pl
from jax.experimental.pallas import tpu as pltpu
from jax.sharding import PartitionSpec as P

MESH = pl.DeviceIdType.MESH
NS = 512
PROBES = 64
J = 4
Y = 4
F32 = jnp.float32
BF16 = jnp.bfloat16


def toeplitz_block(lags, d, sens):
    rows = []
    for b in range(J):
        parts = []
        for c in range(J):
            l = J * d + b - c
            if l < 0:
                parts.append(jnp.zeros((sens, lags.shape[-1]), BF16))
            else:
                parts.append(lags[l // J, l % J])
        rows.append(jnp.concatenate(parts, axis=1))
    return jnp.concatenate(rows, axis=0)


def kernel(
    R, Z, stop,
    probes_ref, lag_ref, weight_ref, mask_ref,
    out_ref, grad_ref,
    pbuf, lbuf, obs, ry, sz, rz, wz, wy, mis, md, send_x, mx, gsend, gbuf,
    local_sem, xs_sem, xr_sem, ps_sem, pr_sem, ys_sem, yr_sem, zs_sem, zr_sem,
    azs_sem, azr_sem, ays_sem, ayr_sem, ds_sem, dr_sem, ms_sem, mr_sem, gs_sem, gr_sem,
):
    r = lax.axis_index("lag")
    c = lax.axis_index("par")
    z, y = c // Y, lax.rem(c, Y)
    x, core = r // 2, lax.rem(r, 2)
    X = R // 2
    sens = NS // R
    npar = pbuf.shape[-1]

    lag_peer = lambda k: (lax.rem(r + k, R), c)
    y_peer = lambda k: (r, z * Y + lax.rem(y + k, Y))
    z_peer = lambda k: (r, lax.rem(z + k, Z) * Y + y)

    barrier = pltpu.get_barrier_semaphore()
    for peer, n in ((lag_peer, R), (y_peer, Y), (z_peer, Z)):
        for k in range(1, n):
            pl.semaphore_signal(barrier, inc=1, device_id=peer(k), device_id_type=MESH)
    pl.semaphore_wait(barrier, R + Y + Z - 3)

    sends = []

    def send(src, dst, ssem, rsem, dev):
        cp = pltpu.make_async_remote_copy(
            src_ref=src, dst_ref=dst, send_sem=ssem, recv_sem=rsem, device_id=dev, device_id_type=MESH
        )
        cp.start()
        sends.append(cp)
        return cp

    own_l = pltpu.make_async_copy(
        lag_ref.at[:, pl.ds(pl.multiple_of(r * sens, sens), sens), :], lbuf.at[r], local_sem.at[0]
    )
    own_p = pltpu.make_async_copy(probes_ref, pbuf.at[r], local_sem.at[1])
    own_l.start()
    own_p.start()
    first = []
    for k in range(1, R):
        q = lax.rem(r + k, R)
        first.append(send(probes_ref, pbuf.at[r], ps_sem.at[k], pr_sem.at[k], (q, c)))
        first.append(
            send(
                lag_ref.at[:, pl.ds(pl.multiple_of(q * sens, sens), sens), :],
                lbuf.at[r], xs_sem.at[k], xr_sem.at[k], (q, c),
            )
        )
    own_l.wait()
    own_p.wait()
    for cp in first:
        cp.wait_recv()

    if stop >= 1:
        for d in range(R):
            n = R - d
            lhs = jnp.concatenate([pbuf[:n, b].reshape(n * PROBES, npar) for b in range(J)], axis=1)
            rhs = toeplitz_block(lbuf, d, sens)
            term = lax.dot_general(lhs, rhs, (((1,), (1,)), ((), ())), preferred_element_type=F32)
            if d == 0:
                obs[...] = term
            else:
                obs[d * PROBES :, :] += term

    rows_y = obs.shape[0] // Y
    if stop >= 2:
        cps = []
        for k in range(1, Y):
            t = lax.rem(y + k, Y)
            cps.append(
                send(
                    obs.at[pl.ds(pl.multiple_of(t * rows_y, rows_y), rows_y), :],
                    ry.at[k - 1], ys_sem.at[k], yr_sem.at[k], y_peer(k),
                )
            )
        total = obs[pl.ds(pl.multiple_of(y * rows_y, rows_y), rows_y), :]
        for k in range(1, Y):
            cps[k - 1].wait_recv()
            total = total + ry[k - 1]
        for i in range(Z):
            sz[i] = total[16 * (i // 2) : 16 * (i // 2) + 16, 128 * (i % 2) : 128 * (i % 2) + 128]
    if stop >= 3:
        cps = []
        for k in range(1, Z):
            cps.append(
                send(sz.at[lax.rem(z + k, Z)], rz.at[k - 1], zs_sem.at[k], zr_sem.at[k], z_peer(k))
            )
        total = sz[z]
        for k in range(1, Z):
            cps[k - 1].wait_recv()
            total = total + rz[k - 1]

    half = 128 // sens
    row = weight_ref[pl.ds(r // half, 1), :] * mask_ref[pl.ds(r // half, 1), :].astype(F32)
    raw = weight_ref[pl.ds(r // half, 1), :]
    on = mask_ref[pl.ds(r // half, 1), :].astype(F32)

    def mine(v):
        swapped = jnp.concatenate([v[:, sens:], v[:, :sens]], axis=1)
        v = jnp.where(lax.rem(r, half) == 0, v, swapped)
        return v

    def both(v):
        return jnp.concatenate([v[:, :sens], v[:, :sens]], axis=1)

    if stop >= 4:
        wz[z] = (both(mine(row)) * total).astype(BF16)
        cps = []
        for k in range(1, Z):
            cps.append(send(wz.at[z], wz.at[z], azs_sem.at[k], azr_sem.at[k], z_peer(k)))
        for cp in cps:
            cp.wait_recv()
    if stop >= 5:
        cps = []
        for k in range(1, Y):
            cps.append(send(wz, wy.at[y], ays_sem.at[k], ayr_sem.at[k], y_peer(k)))
        wy[y] = wz[...]
        for cp in cps:
            cp.wait_recv()

    if stop >= 6:
        tot = jnp.zeros((1, 128), F32)
        for i in range(Y):
            for j in range(Z):
                w = wy[i, j].astype(F32)
                tot = tot + jnp.sum(w * w, axis=0, keepdims=True)
        tot = tot[:, :sens] + tot[:, sens:]
        wr = mine(raw)[:, :sens]
        g = mine(on)[:, :sens] * tot / (wr * wr) * (1.0 / (R * J * PROBES))
        g = jnp.concatenate([g, g], axis=1)
        gsend[...] = jnp.broadcast_to(g, (8, 128))
        gcps = []
        for k in range(1, R):
            gcps.append(send(gsend, gbuf.at[r], gs_sem.at[k], gr_sem.at[k], lag_peer(k)))
        gbuf[r] = gsend[...]

        def wrow(a):
            i, h = a * PROBES // rows_y, (a * PROBES % rows_y) // 16
            return jnp.concatenate(
                [jnp.concatenate([wy[i, 2 * (h + q)], wy[i, 2 * (h + q) + 1]], axis=1) for q in range(PROBES // 16)],
                axis=0,
            )

        wfull = [wrow(a) for a in range(R)]
        for d in range(R):
            n = R - d
            lhs = jnp.concatenate(wfull[d:], axis=0)
            rhs = toeplitz_block(lbuf, d, sens)
            term = jnp.dot(lhs, rhs, preferred_element_type=F32)
            for a in range(n):
                piece = term[a * PROBES : (a + 1) * PROBES]
                if d == 0:
                    mis[a % 2, a // 2] = piece
                else:
                    mis[a % 2, a // 2] += piece

    if stop >= 7:
        other = r + 1 - 2 * core
        cp = send(mis.at[1 - core], md, ds_sem, dr_sem, (other, c))
        cp.wait_recv()
        for i in range(X):
            send_x[i] = mis[core, i] + md[i]
    if stop >= 8:
        cps = []
        for k in range(1, X):
            t = lax.rem(x + k, X)
            cps.append(
                send(send_x.at[t], mx.at[k - 1], ms_sem.at[k], mr_sem.at[k], (t * 2 + core, c))
            )
        total = send_x[x]
        for k in range(1, X):
            cps[k - 1].wait_recv()
            total = total + mx[k - 1]
        for b in range(J):
            out_ref[b] = total[:, b * npar : (b + 1) * npar] + pbuf[r, b].astype(F32)
        for cp in gcps:
            cp.wait_recv()
        for q in range(R // 2):
            grad_ref[q : q + 1, :] = jnp.concatenate(
                [gbuf[2 * q, 0:1, :sens], gbuf[2 * q + 1, 0:1, :sens]], axis=1
            )
    elif stop >= 6:
        for cp in gcps:
            cp.wait_recv()
    if stop < 8:
        out_ref[...] = jnp.zeros_like(out_ref)
        grad_ref[...] = jnp.zeros_like(grad_ref)
    for cp in sends:
        cp.wait_send()


def per_device(R, Z, stop, probes, lag_blocks, sensor_weights, sensor_mask):
    npar = probes.shape[2]
    sens = NS // R
    rows, lanes = R * PROBES, J * sens
    X = R // 2
    dma = lambda n: pltpu.SemaphoreType.DMA((n,))
    out, grad = pl.pallas_call(
        functools.partial(kernel, R, Z, stop),
        out_shape=(
            jax.ShapeDtypeStruct((J, PROBES, npar), F32),
            jax.ShapeDtypeStruct((NS // 128, 128), F32),
        ),
        in_specs=[pl.BlockSpec(memory_space=pl.ANY)] * 2 + [pl.BlockSpec(memory_space=pltpu.VMEM)] * 2,
        out_specs=(pl.BlockSpec(memory_space=pltpu.VMEM),) * 2,
        scratch_shapes=[
            pltpu.VMEM((R, J, PROBES, npar), BF16),
            pltpu.VMEM((R, J, sens, npar), BF16),
            pltpu.VMEM((rows, lanes), F32),
            pltpu.VMEM((Y - 1, rows // Y, lanes), F32),
            pltpu.VMEM((Z, 16, 128), F32),
            pltpu.VMEM((Z - 1, 16, 128), F32),
            pltpu.VMEM((Z, 16, 128), BF16),
            pltpu.VMEM((Y, Z, 16, 128), BF16),
            pltpu.VMEM((2, X, PROBES, J * npar), F32),
            pltpu.VMEM((X, PROBES, J * npar), F32),
            pltpu.VMEM((X, PROBES, J * npar), F32),
            pltpu.VMEM((X - 1, PROBES, J * npar), F32),
            pltpu.VMEM((8, 128), F32),
            pltpu.VMEM((R, 8, 128), F32),
            dma(2), dma(R), dma(R), dma(R), dma(R), dma(Y), dma(Y), dma(Z), dma(Z),
            dma(Z), dma(Z), dma(Y), dma(Y),
            pltpu.SemaphoreType.DMA, pltpu.SemaphoreType.DMA, dma(X), dma(X), dma(R), dma(R),
        ],
        compiler_params=pltpu.CompilerParams(
            collective_id=0, has_side_effects=True, vmem_limit_bytes=48 * 1024 * 1024
        ),
        cost_estimate=pl.CostEstimate(flops=2 * 10**9, bytes_accessed=10**6, transcendentals=0),
        name="toeplitz",
    )(
        probes, lag_blocks,
        sensor_weights.reshape(NS // 128, 128), sensor_mask.reshape(NS // 128, 128),
    )
    return out, grad.reshape(NS)


def solution(mesh, stop=8):
    R, Z = mesh.shape["lag"], mesh.shape["par"] // Y
    return jax.shard_map(
        functools.partial(per_device, R, Z, stop),
        mesh=mesh,
        in_specs=(P("lag", None, "par"), P("lag", None, "par"), P(), P()),
        out_specs=(P("lag", None, "par"), P()),
        check_vma=False,
    )
```

```python
import functools

import jax
import jax.numpy as jnp
from jax import lax
from jax.experimental import pallas as pl
from jax.experimental.pallas import tpu as pltpu
from jax.sharding import PartitionSpec as P

MESH = pl.DeviceIdType.MESH
NS = 512
PROBES = 64
J = 4
Y = 4
Z = 16
H = 2
Q = 4
F32 = jnp.float32
BF16 = jnp.bfloat16


def toeplitz_block(lags, d):
    rows = []
    for b in range(J):
        parts = []
        for c in range(J):
            l = J * d + b - c
            if l < 0:
                parts.append(jnp.zeros(lags.shape[-2:], BF16))
            else:
                parts.append(lags[l // J, l % J])
        rows.append(jnp.concatenate(parts, axis=1))
    return jnp.concatenate(rows, axis=0)


def kernel(
    R, stop,
    probes_ref, lag_ref, weight_hbm, mask_hbm,
    out_ref, grad_ref,
    pbuf, lbuf, weight_ref, mask_ref, obs, ry, sz, rz, wz, wy, mis, md, send_x, mx, gsend, gbuf,
    near_sem, local_sem, ps_sem, pr_sem, fs_sem, fr_sem, xs_sem, xr_sem, ys_sem, yr_sem,
    zs_sem, zr_sem, azs_sem, azr_sem, ays_sem, ayr_sem, ds_sem, dr_sem, ms_sem, mr_sem, gs_sem, gr_sem,
):
    r = lax.axis_index("lag")
    c = lax.axis_index("par")
    z, y = c // Y, lax.rem(c, Y)
    zq = z // Q
    x, core = r // 2, lax.rem(r, 2)
    X = R // 2
    sens = NS // R
    part = sens // H
    npar = pbuf.shape[-1]
    partner = (r + 1 - 2 * core, c)

    lag_peer = lambda k: (lax.rem(r + k, R), c)
    x_peer = lambda k: (lax.rem(x + k, X) * 2 + core, c)
    y_peer = lambda k: (r, z * Y + lax.rem(y + k, Y))
    z_at = lambda t: (r, t * Y + y)
    z_peer = lambda k: z_at(lax.rem(z + k + Z, Z))

    def signal(sem, dev):
        pl.semaphore_signal(sem, inc=1, device_id=dev, device_id_type=MESH)

    def remote(src, dst, ssem, rsem, dev):
        return pltpu.make_async_remote_copy(
            src_ref=src, dst_ref=dst, send_sem=ssem, recv_sem=rsem, device_id=dev, device_id_type=MESH
        )

    sends = []

    def send(*a):
        cp = remote(*a)
        cp.start()
        sends.append(cp)
        return cp

    local = [
        pltpu.make_async_copy(probes_ref, pbuf.at[r], local_sem.at[0]),
        pltpu.make_async_copy(weight_hbm, weight_ref, local_sem.at[1]),
        pltpu.make_async_copy(mask_hbm, mask_ref, local_sem.at[2]),
    ]

    def lag_part(q, h):
        return lag_ref.at[:, pl.ds(pl.multiple_of(q * sens + h * part, part), part), :]

    for h in range(H):
        local.append(pltpu.make_async_copy(lag_part(r, h), lbuf.at[h, r], local_sem.at[3 + h]))
    for cp in local:
        cp.start()

    barrier = pltpu.get_barrier_semaphore()
    for k in range(1, R):
        signal(barrier, lag_peer(k))
    for k in range(1, Y):
        signal(barrier, y_peer(k))
    for k in (1, -1):
        signal(barrier, z_peer(k))
    pl.semaphore_wait(barrier, R + Y)

    def near_signal(i):
        for k in (1 << i, -(1 << i)):
            signal(near_sem.at[i], z_peer(k))

    def near_wait(i):
        pl.semaphore_wait(near_sem.at[i], 2)

    near_signal(0)

    pcps = [send(probes_ref, pbuf.at[r], ps_sem.at[0], pr_sem.at[0], partner)]
    for k in (2, 1, 3):
        pcps.append(send(probes_ref, pbuf.at[r], ps_sem.at[k], pr_sem.at[k], x_peer(k)))
    lcps = [[], []]
    for h in range(H):
        for k in (4, 5, 3, 2, 6, 7, 1):
            q = lax.rem(r + k, R)
            lcps[h].append(send(lag_part(q, h), lbuf.at[h, r], xs_sem.at[h, k], xr_sem.at[h, k], (q, c)))
    near_wait(0)
    near_signal(1)
    fcps = []
    for k in (1, 3, 2):
        pcps[{2: 1, 1: 2, 3: 3}[k]].wait_recv()
        src = lax.rem(x - k + X, X) * 2 + core
        fcps.append(send(pbuf.at[src], pbuf.at[src], fs_sem.at[k], fr_sem.at[k], partner))
    near_wait(1)
    near_signal(2)
    for cp in local:
        cp.wait()
    pcps[0].wait_recv()
    for cp in fcps:
        cp.wait_recv()

    rows_y = R * PROBES // Y
    rows_q = rows_y // Q

    def forward(h):
        for cp in lcps[h]:
            cp.wait_recv()
        for d in range(R):
            n = R - d
            lhs = jnp.concatenate([pbuf[:n, b].reshape(n * PROBES, npar) for b in range(J)], axis=1)
            term = lax.dot_general(
                lhs, toeplitz_block(lbuf.at[h], d), (((1,), (1,)), ((), ())), preferred_element_type=F32
            )
            if d == 0:
                obs[h] = term
            else:
                obs[h, d * PROBES :, :] += term

    def quarter(o):
        return lax.rem(zq + o, Q)

    order = (2, 1, 3, 0)

    def sum_y_start(h):
        cps = []
        for i, o in enumerate(order):
            q = quarter(o)
            for k in range(1, Y):
                t = lax.rem(y + k, Y)
                cps.append(
                    send(
                        obs.at[h, pl.ds(pl.multiple_of(t * rows_y + q * rows_q, rows_q), rows_q), :],
                        ry.at[h, i, k - 1], ys_sem.at[h, i, k], yr_sem.at[h, i, k], y_peer(k),
                    )
                )
        return cps

    late = []

    def sum_z_start(h, ycps):
        for i, o in enumerate(order):
            q = quarter(o)
            total = obs[h, pl.ds(pl.multiple_of(y * rows_y + q * rows_q, rows_q), rows_q), :]
            for k in range(1, Y):
                ycps[i * (Y - 1) + k - 1].wait_recv()
                total = total + ry[h, i, k - 1]
            sz[h, i] = total
            for e in range(2):
                t = Q * q + 2 * e + h
                k = lax.rem(t - z + Z, Z)
                cp = remote(
                    sz.at[h, i, pl.ds(16 * e, 16), :], rz.at[k],
                    zs_sem.at[h, i, e], zr_sem.at[k], z_at(t),
                )
                if o:
                    cp.start()
                    sends.append(cp)
                else:
                    pl.when(t != z)(cp.start)
                    late.append((t != z, cp))

    forward(0)
    ycps0 = sum_y_start(0)
    forward(1)
    ycps1 = sum_y_start(1)
    near_wait(2)
    sum_z_start(0, ycps0)
    sum_z_start(1, ycps1)

    hz = lax.rem(z, H)
    row = weight_ref[pl.ds(r // 2, 1), :]
    on = mask_ref[pl.ds(r // 2, 1), :].astype(F32)
    own = sz[hz, 3, pl.ds(pl.multiple_of(16 * (lax.rem(z, Q) // 2), 16), 16), :]
    for k in range(1, Z):
        remote(rz.at[k], rz.at[k], zs_sem.at[0, 0, 0], zr_sem.at[k], z_peer(k)).wait_recv()
        own = own + rz[k]
    both = row * on
    scale = jnp.zeros((1, 128), F32)
    for j in range(4):
        piece = both[:, j * part : (j + 1) * part]
        piece = jnp.concatenate([piece] * J, axis=1)
        scale = jnp.where(core * H + hz == j, piece, scale)
    wz[z] = (scale * own).astype(BF16)
    for k in (8, 7, 9, 6, 10, 5, 11, 4, 12, 3, 13, 2, 14, 1, 15):
        send(wz.at[z], wz.at[z], azs_sem.at[k], azr_sem.at[z], z_peer(k))
    aycps = []
    for i, o in enumerate((0, 1, 3, 2)):
        q = quarter(o)
        for e in range(Q):
            t = Q * q + e
            cp = remote(wz.at[t], wz.at[t], azs_sem.at[1], azr_sem.at[t], z_at(t))
            if o:
                cp.wait_recv()
            else:
                pl.when(t != z)(cp.wait_recv)
        rng = pl.ds(Q * q, Q)
        for k in range(1, Y):
            aycps.append(send(wz.at[rng], wy.at[y, rng], ays_sem.at[i, k], ayr_sem.at[i, k], y_peer(k)))
    wy[y] = wz[...]
    for cp in aycps:
        cp.wait_recv()

    def wrow(a):
        i, g = a * PROBES // rows_y, (a * PROBES % rows_y) // 16
        return jnp.concatenate(
            [jnp.concatenate([wy[i, 2 * (g + q)], wy[i, 2 * (g + q) + 1]], axis=1) for q in range(PROBES // 16)],
            axis=0,
        )

    wfull = [wrow(a) for a in range(R)]
    for d in range(R):
        n = R - d
        rhs = jnp.concatenate([toeplitz_block(lbuf.at[h], d) for h in range(H)], axis=0)
        term = jnp.dot(jnp.concatenate(wfull[d:], axis=0), rhs, preferred_element_type=F32)
        for a in range(n):
            piece = term[a * PROBES : (a + 1) * PROBES]
            if d == 0:
                mis[a % 2, a // 2] = piece
            else:
                mis[a % 2, a // 2] += piece

    dcps = []
    for k in (2, 1, 3, 0):
        t = lax.rem(x + k, X)
        dcps.append(send(mis.at[1 - core, t], md.at[k], ds_sem.at[k], dr_sem.at[k], partner))

    def mine(v):
        return jnp.where(core == 0, v[:, :sens], v[:, sens:])

    tot = [jnp.zeros((16, 128), F32) for _ in range(H)]
    for i in range(Y):
        for j in range(Z):
            w = wy[i, j].astype(F32)
            tot[j % H] = tot[j % H] + w * w
    sq = []
    for h in range(H):
        v = jnp.sum(tot[h], axis=0, keepdims=True)
        sq.append(sum(v[:, b * part : (b + 1) * part] for b in range(J)))
    sq = jnp.concatenate(sq, axis=1)
    wr = mine(row)
    g = mine(on) * sq / (wr * wr) * (1.0 / (R * J * PROBES))
    gsend[...] = jnp.broadcast_to(jnp.concatenate([g, g], axis=1), (8, 128))
    gcps = []
    for k in range(1, R):
        gcps.append(send(gsend, gbuf.at[r], gs_sem.at[k], gr_sem.at[k], lag_peer(k)))
    gbuf[r] = gsend[...]

    mcps = []
    for i, k in enumerate((2, 1, 3)):
        t = lax.rem(x + k, X)
        dcps[i].wait_recv()
        send_x[k] = (mis[core, t] + md[k]).astype(BF16)
        mcps.append(send(send_x.at[k], mx.at[k], ms_sem.at[k], mr_sem.at[k], x_peer(k)))
    dcps[3].wait_recv()
    total = mis[core, x] + md[0]
    total = total + jnp.concatenate([pbuf[r, b].astype(F32) for b in range(J)], axis=1)
    for i, k in ((1, 1), (2, 3), (0, 2)):
        mcps[i].wait_recv()
        total = total + mx[k].astype(F32)
    for b in range(J):
        out_ref[b] = total[:, b * npar : (b + 1) * npar]
    for cp in gcps:
        cp.wait_recv()
    for q in range(R // 2):
        grad_ref[q : q + 1, :] = jnp.concatenate([gbuf[2 * q, 0:1, :sens], gbuf[2 * q + 1, 0:1, :sens]], axis=1)
    for cp in sends:
        cp.wait_send()
    for cond, cp in late:
        pl.when(cond)(cp.wait_send)


def per_device(R, stop, probes, lag_blocks, sensor_weights, sensor_mask):
    npar = probes.shape[2]
    sens = NS // R
    part = sens // H
    rows = R * PROBES
    X = R // 2
    dma = lambda *n: pltpu.SemaphoreType.DMA(n)
    out, grad = pl.pallas_call(
        functools.partial(kernel, R, stop),
        out_shape=(
            jax.ShapeDtypeStruct((J, PROBES, npar), F32),
            jax.ShapeDtypeStruct((NS // 128, 128), F32),
        ),
        in_specs=[pl.BlockSpec(memory_space=pltpu.HBM)] * 4,
        out_specs=(pl.BlockSpec(memory_space=pltpu.VMEM),) * 2,
        scratch_shapes=[
            pltpu.VMEM((R, J, PROBES, npar), BF16),
            pltpu.VMEM((H, R, J, part, npar), BF16),
            pltpu.VMEM((NS // 128, 128), F32),
            pltpu.VMEM((NS // 128, 128), jnp.int32),
            pltpu.VMEM((H, rows, 128), F32),
            pltpu.VMEM((H, Q, Y - 1, rows // Y // Q, 128), F32),
            pltpu.VMEM((H, Q, rows // Y // Q, 128), F32),
            pltpu.VMEM((Z, 16, 128), F32),
            pltpu.VMEM((Z, 16, 128), BF16),
            pltpu.VMEM((Y, Z, 16, 128), BF16),
            pltpu.VMEM((2, X, PROBES, J * npar), F32),
            pltpu.VMEM((X, PROBES, J * npar), F32),
            pltpu.VMEM((X, PROBES, J * npar), BF16),
            pltpu.VMEM((X, PROBES, J * npar), BF16),
            pltpu.VMEM((8, 128), F32),
            pltpu.VMEM((R, 8, 128), F32),
            pltpu.SemaphoreType.REGULAR((3,)),
            dma(5), dma(X), dma(X), dma(X), dma(X), dma(H, R), dma(H, R), dma(H, Q, Y), dma(H, Q, Y),
            dma(H, Q, 2), dma(Z), dma(Z), dma(Z), dma(Q, Y), dma(Q, Y), dma(X), dma(X), dma(X), dma(X),
            dma(R), dma(R),
        ],
        compiler_params=pltpu.CompilerParams(
            collective_id=0, has_side_effects=True, vmem_limit_bytes=48 * 1024 * 1024
        ),
        cost_estimate=pl.CostEstimate(flops=2 * 10**9, bytes_accessed=10**6, transcendentals=0),
        name="toeplitz",
    )(
        probes, lag_blocks,
        sensor_weights.reshape(NS // 128, 128), sensor_mask.reshape(NS // 128, 128),
    )
    return out, grad.reshape(NS)


def solution(mesh, stop=8):
    R = mesh.shape["lag"]
    return jax.shard_map(
        functools.partial(per_device, R, stop),
        mesh=mesh,
        in_specs=(P("lag", None, "par"), P("lag", None, "par"), P(), P()),
        out_specs=(P("lag", None, "par"), P()),
        check_vma=False,
    )
```

```python
import functools

import jax
import jax.numpy as jnp
from jax import lax
from jax.experimental import pallas as pl
from jax.experimental.pallas import tpu as pltpu
from jax.sharding import PartitionSpec as P

MESH = pl.DeviceIdType.MESH
NS = 512
PROBES = 64
J = 4
Y = 4
Z = 16
H = 2
Q = 4
F32 = jnp.float32
BF16 = jnp.bfloat16


def toeplitz_block(lags, d):
    rows = []
    for b in range(J):
        parts = []
        for c in range(J):
            l = J * d + b - c
            if l < 0:
                parts.append(jnp.zeros(lags.shape[-2:], BF16))
            else:
                parts.append(lags[l // J, l % J])
        rows.append(jnp.concatenate(parts, axis=1))
    return jnp.concatenate(rows, axis=0)


def kernel(
    R, stop,
    probes_ref, lag_ref, weight_hbm, mask_hbm,
    out_ref, grad_ref,
    pbuf, lbuf, weight_ref, mask_ref, obs, ry, sz, rz, wz, wy, mis, md, send_x, mx, gsend, gbuf,
    near_sem, local_sem, ps_sem, pr_sem, fs_sem, fr_sem, xs_sem, xr_sem, ys_sem, yr_sem,
    zs_sem, zr_sem, azs_sem, azr_sem, ays_sem, ayr_sem, ds_sem, dr_sem, ms_sem, mr_sem, gs_sem, gr_sem,
):
    r = lax.axis_index("lag")
    c = lax.axis_index("par")
    z, y = c // Y, lax.rem(c, Y)
    zq = z // Q
    x, core = r // 2, lax.rem(r, 2)
    X = R // 2
    sens = NS // R
    part = sens // H
    npar = pbuf.shape[-1]
    partner = (r + 1 - 2 * core, c)

    lag_peer = lambda k: (lax.rem(r + k, R), c)
    x_peer = lambda k: (lax.rem(x + k, X) * 2 + core, c)
    y_peer = lambda k: (r, z * Y + lax.rem(y + k, Y))
    z_at = lambda t: (r, t * Y + y)
    z_peer = lambda k: z_at(lax.rem(z + k + Z, Z))

    def signal(sem, dev):
        pl.semaphore_signal(sem, inc=1, device_id=dev, device_id_type=MESH)

    def remote(src, dst, ssem, rsem, dev):
        return pltpu.make_async_remote_copy(
            src_ref=src, dst_ref=dst, send_sem=ssem, recv_sem=rsem, device_id=dev, device_id_type=MESH
        )

    sends = []

    def send(*a):
        cp = remote(*a)
        cp.start()
        sends.append(cp)
        return cp

    local = [
        pltpu.make_async_copy(probes_ref, pbuf.at[r], local_sem.at[0]),
        pltpu.make_async_copy(weight_hbm, weight_ref, local_sem.at[1]),
        pltpu.make_async_copy(mask_hbm, mask_ref, local_sem.at[2]),
    ]

    def lag_part(q, h):
        return lag_ref.at[:, pl.ds(pl.multiple_of(q * sens + h * part, part), part), :]

    for h in range(H):
        local.append(pltpu.make_async_copy(lag_part(r, h), lbuf.at[h, r], local_sem.at[3 + h]))
    for cp in local:
        cp.start()

    barrier = pltpu.get_barrier_semaphore()
    for k in range(1, R):
        signal(barrier, lag_peer(k))
    for k in range(1, Y):
        signal(barrier, y_peer(k))
    for k in (1, -1):
        signal(barrier, z_peer(k))
    pl.semaphore_wait(barrier, R + Y)

    def near_signal(i):
        for k in (1 << i, -(1 << i)):
            signal(near_sem.at[i], z_peer(k))

    def near_wait(i):
        pl.semaphore_wait(near_sem.at[i], 2)

    near_signal(0)

    pcps = [send(probes_ref, pbuf.at[r], ps_sem.at[0], pr_sem.at[0], partner)]
    for k in (2, 1, 3):
        pcps.append(send(probes_ref, pbuf.at[r], ps_sem.at[k], pr_sem.at[k], x_peer(k)))
    lcps = [[], []]
    for h in range(H):
        for k in (4, 5, 3, 2, 6, 7, 1):
            q = lax.rem(r + k, R)
            lcps[h].append(send(lag_part(q, h), lbuf.at[h, r], xs_sem.at[h, k], xr_sem.at[h, k], (q, c)))
    near_wait(0)
    near_signal(1)
    fcps = []
    for k in (1, 3, 2):
        pcps[{2: 1, 1: 2, 3: 3}[k]].wait_recv()
        src = lax.rem(x - k + X, X) * 2 + core
        fcps.append(send(pbuf.at[src], pbuf.at[src], fs_sem.at[k], fr_sem.at[k], partner))
    near_wait(1)
    near_signal(2)
    for cp in local:
        cp.wait()
    pcps[0].wait_recv()
    for cp in fcps:
        cp.wait_recv()

    rows = PROBES // Q

    def forward(h, start, count):
        acc = None
        for d in range(R):
            n = R - d
            lhs = jnp.concatenate(
                [pbuf[:n, b, pl.ds(start, count), :].reshape(n * count, npar) for b in range(J)], axis=1
            )
            term = lax.dot_general(
                lhs, toeplitz_block(lbuf.at[h], d), (((1,), (1,)), ((), ())), preferred_element_type=F32
            ).reshape(n, count, 128)
            if d == 0:
                acc = [term[a] for a in range(R)]
            else:
                for a in range(n):
                    acc[a + d] = acc[a + d] + term[a]
        for a in range(R):
            obs[h, a, pl.ds(start, count), :] = acc[a]

    def quarter(o):
        return lax.rem(zq + o, Q)

    def probes_of(q):
        return pl.ds(pl.multiple_of(q * rows, rows), rows)

    order = (2, 1, 3, 0)

    def sum_y_start(h, i):
        q = quarter(order[i])
        cps = []
        for k in range(1, Y):
            t = lax.rem(y + k, Y)
            cps.append(
                send(
                    obs.at[h, pl.ds(2 * t, 2), probes_of(q), :],
                    ry.at[h, i, k - 1], ys_sem.at[h, i, k], yr_sem.at[h, i, k], y_peer(k),
                )
            )
        return cps

    late = []

    def sum_z_start(h, i, ycps):
        o = order[i]
        q = quarter(o)
        total = obs[h, pl.ds(2 * y, 2), probes_of(q), :]
        for k in range(1, Y):
            ycps[k - 1].wait_recv()
            total = total + ry[h, i, k - 1]
        sz[h, i] = total
        for e in range(2):
            t = Q * q + 2 * e + h
            k = lax.rem(t - z + Z, Z)
            cp = remote(sz.at[h, i, e], rz.at[k], zs_sem.at[h, i, e], zr_sem.at[k], z_at(t))
            if o:
                cp.start()
                sends.append(cp)
            else:
                pl.when(t != z)(cp.start)
                late.append((t != z, cp))

    for cp in lcps[0]:
        cp.wait_recv()
    forward(0, 0, PROBES)
    ycps = [[sum_y_start(0, i) for i in range(Q)], []]
    for cp in lcps[1]:
        cp.wait_recv()
    for i in range(Q):
        forward(1, quarter(order[i]) * rows, rows)
        ycps[1].append(sum_y_start(1, i))
    near_wait(2)
    for h in range(H):
        for i in range(Q):
            sum_z_start(h, i, ycps[h][i])

    hz = lax.rem(z, H)
    row = weight_ref[pl.ds(r // 2, 1), :]
    on = mask_ref[pl.ds(r // 2, 1), :].astype(F32)
    own = sz[hz, 3, lax.rem(z, Q) // 2]
    for k in range(1, Z):
        remote(rz.at[k], rz.at[k], zs_sem.at[0, 0, 0], zr_sem.at[k], z_peer(k)).wait_recv()
        own = own + rz[k]
    both = row * on
    scale = jnp.zeros((1, 128), F32)
    for j in range(4):
        piece = both[:, j * part : (j + 1) * part]
        piece = jnp.concatenate([piece] * J, axis=1)
        scale = jnp.where(core * H + hz == j, piece, scale)
    wz[z] = (scale * own).astype(BF16)
    for k in (8, 7, 9, 6, 10, 5, 11, 4, 12, 3, 13, 2, 14, 1, 15):
        send(wz.at[z], wz.at[z], azs_sem.at[k], azr_sem.at[z], z_peer(k))
    arrive = (0, 1, 3, 2)
    aycps = []
    for i, o in enumerate(arrive):
        q = quarter(o)
        for e in range(Q):
            t = Q * q + e
            cp = remote(wz.at[t], wz.at[t], azs_sem.at[1], azr_sem.at[t], z_at(t))
            if o:
                cp.wait_recv()
            else:
                pl.when(t != z)(cp.wait_recv)
        aycps.append([])
        for k in range(1, Y):
            aycps[i].append(
                send(wz.at[pl.ds(Q * q, Q)], wy.at[q, y], ays_sem.at[i, k], ayr_sem.at[i, k], y_peer(k))
            )
        wy[q, y] = wz[pl.ds(Q * q, Q)]

    tot = [jnp.zeros((rows, 128), F32) for _ in range(H)]
    half = J * npar // 2

    def adjoint(i):
        q = quarter(arrive[i])
        for cp in aycps[i]:
            cp.wait_recv()
        w = []
        for a in range(R):
            e = 2 * (a % 2)
            w.append(jnp.concatenate([wy[q, a // 2, e], wy[q, a // 2, e + 1]], axis=1))
        for u in range(2):
            acc = None
            for d in range(R):
                n = R - d
                rhs = jnp.concatenate(
                    [toeplitz_block(lbuf.at[h], d)[:, u * half : (u + 1) * half] for h in range(H)], axis=0
                )
                term = jnp.dot(jnp.concatenate(w[d:], axis=0), rhs, preferred_element_type=F32)
                pieces = [term[a * rows : (a + 1) * rows] for a in range(n)]
                acc = pieces if d == 0 else [acc[a] + pieces[a] for a in range(n)] + acc[n:]
            for a in range(R):
                mis[i, a % 2, a // 2, :, u * half : (u + 1) * half] = acc[a]
        cps = []
        for k in (2, 1, 3, 0):
            t = lax.rem(x + k, X)
            cps.append(
                send(mis.at[i, 1 - core, t], md.at[i, k], ds_sem.at[i, k], dr_sem.at[i, k], partner)
            )
        for a in range(R):
            for h in range(H):
                v = w[a][:, 128 * h : 128 * h + 128].astype(F32)
                tot[h] = tot[h] + v * v
        return cps

    def sum_x_start(i, dcps):
        cps = []
        for n, k in enumerate((2, 1, 3)):
            t = lax.rem(x + k, X)
            dcps[n].wait_recv()
            send_x[i, k] = (mis[i, core, t] + md[i, k]).astype(BF16)
            cps.append(send(send_x.at[i, k], mx.at[i, k], ms_sem.at[i, k], mr_sem.at[i, k], x_peer(k)))
        return cps

    dcps, mcps = [], []
    for i in range(Q):
        dcps.append(adjoint(i))
        if i:
            mcps.append(sum_x_start(i - 1, dcps[i - 1]))

    def mine(v):
        return jnp.where(core == 0, v[:, :sens], v[:, sens:])

    sq = []
    for h in range(H):
        v = jnp.sum(tot[h], axis=0, keepdims=True)
        sq.append(sum(v[:, b * part : (b + 1) * part] for b in range(J)))
    sq = jnp.concatenate(sq, axis=1)
    wr = mine(row)
    g = mine(on) * sq / (wr * wr) * (1.0 / (R * J * PROBES))
    gsend[...] = jnp.broadcast_to(jnp.concatenate([g, g], axis=1), (8, 128))
    gcps = []
    for k in range(1, R):
        gcps.append(send(gsend, gbuf.at[r], gs_sem.at[k], gr_sem.at[k], lag_peer(k)))
    gbuf[r] = gsend[...]

    mcps.append(sum_x_start(Q - 1, dcps[Q - 1]))
    for i in range(Q):
        at = probes_of(quarter(arrive[i]))
        dcps[i][3].wait_recv()
        total = mis[i, core, x] + md[i, 0]
        total = total + jnp.concatenate([pbuf[r, b, at, :].astype(F32) for b in range(J)], axis=1)
        for n, k in ((1, 1), (2, 3), (0, 2)):
            mcps[i][n].wait_recv()
            total = total + mx[i, k].astype(F32)
        for b in range(J):
            out_ref[b, at, :] = total[:, b * npar : (b + 1) * npar]
    for cp in gcps:
        cp.wait_recv()
    for q in range(R // 2):
        grad_ref[q : q + 1, :] = jnp.concatenate([gbuf[2 * q, 0:1, :sens], gbuf[2 * q + 1, 0:1, :sens]], axis=1)
    for cp in sends:
        cp.wait_send()
    for cond, cp in late:
        pl.when(cond)(cp.wait_send)


def per_device(R, stop, probes, lag_blocks, sensor_weights, sensor_mask):
    npar = probes.shape[2]
    sens = NS // R
    part = sens // H
    X = R // 2
    dma = lambda *n: pltpu.SemaphoreType.DMA(n)
    out, grad = pl.pallas_call(
        functools.partial(kernel, R, stop),
        out_shape=(
            jax.ShapeDtypeStruct((J, PROBES, npar), F32),
            jax.ShapeDtypeStruct((NS // 128, 128), F32),
        ),
        in_specs=[pl.BlockSpec(memory_space=pltpu.HBM)] * 4,
        out_specs=(pl.BlockSpec(memory_space=pltpu.VMEM),) * 2,
        scratch_shapes=[
            pltpu.VMEM((R, J, PROBES, npar), BF16),
            pltpu.VMEM((H, R, J, part, npar), BF16),
            pltpu.VMEM((NS // 128, 128), F32),
            pltpu.VMEM((NS // 128, 128), jnp.int32),
            pltpu.VMEM((H, R, PROBES, 128), F32),
            pltpu.VMEM((H, Q, Y - 1, 2, PROBES // Q, 128), F32),
            pltpu.VMEM((H, Q, 2, PROBES // Q, 128), F32),
            pltpu.VMEM((Z, 16, 128), F32),
            pltpu.VMEM((Z, 16, 128), BF16),
            pltpu.VMEM((Q, Y, Q, 16, 128), BF16),
            pltpu.VMEM((Q, 2, X, PROBES // Q, J * npar), F32),
            pltpu.VMEM((Q, X, PROBES // Q, J * npar), F32),
            pltpu.VMEM((Q, X, PROBES // Q, J * npar), BF16),
            pltpu.VMEM((Q, X, PROBES // Q, J * npar), BF16),
            pltpu.VMEM((8, 128), F32),
            pltpu.VMEM((R, 8, 128), F32),
            pltpu.SemaphoreType.REGULAR((3,)),
            dma(5), dma(X), dma(X), dma(X), dma(X), dma(H, R), dma(H, R), dma(H, Q, Y), dma(H, Q, Y),
            dma(H, Q, 2), dma(Z), dma(Z), dma(Z), dma(Q, Y), dma(Q, Y), dma(Q, X), dma(Q, X), dma(Q, X), dma(Q, X),
            dma(R), dma(R),
        ],
        compiler_params=pltpu.CompilerParams(
            collective_id=0, has_side_effects=True, vmem_limit_bytes=48 * 1024 * 1024
        ),
        cost_estimate=pl.CostEstimate(flops=2 * 10**9, bytes_accessed=10**6, transcendentals=0),
        name="toeplitz",
    )(
        *(
            pltpu.with_memory_space_constraint(v, pltpu.HBM)
            for v in (probes, lag_blocks, sensor_weights.reshape(NS // 128, 128), sensor_mask.reshape(NS // 128, 128))
        )
    )
    return out, grad.reshape(NS)


def solution(mesh, stop=8):
    R = mesh.shape["lag"]
    return jax.shard_map(
        functools.partial(per_device, R, stop),
        mesh=mesh,
        in_specs=(P("lag", None, "par"), P("lag", None, "par"), P(), P()),
        out_specs=(P("lag", None, "par"), P()),
        check_vma=False,
    )
```

```python
import functools

import jax
import jax.numpy as jnp
from jax import lax
from jax.experimental import pallas as pl
from jax.experimental.pallas import tpu as pltpu
from jax.sharding import PartitionSpec as P

MESH = pl.DeviceIdType.MESH
NS = 512
PROBES = 64
J = 4
Y = 4
Z = 16
H = 2
Q = 4
F32 = jnp.float32
BF16 = jnp.bfloat16


def toeplitz_block(lags, d):
    rows = []
    for b in range(J):
        parts = []
        for c in range(J):
            l = J * d + b - c
            if l < 0:
                parts.append(jnp.zeros(lags.shape[-2:], BF16))
            else:
                parts.append(lags[l // J, l % J])
        rows.append(jnp.concatenate(parts, axis=1))
    return jnp.concatenate(rows, axis=0)


def kernel(
    R, stop,
    probes_ref, lag_ref, weight_hbm, mask_hbm,
    out_ref, grad_ref,
    pbuf, lbuf, weight_ref, mask_ref, obs, ry, sz, rz, wz, wy, mis, md, send_x, mx, gsend, gbuf,
    near_sem, local_sem, ps_sem, pr_sem, fs_sem, fr_sem, xs_sem, xr_sem, ys_sem, yr_sem,
    zs_sem, zr_sem, azs_sem, azr_sem, ays_sem, ayr_sem, ds_sem, dr_sem, ms_sem, mr_sem, gs_sem, gr_sem,
):
    r = lax.axis_index("lag")
    c = lax.axis_index("par")
    z, y = c // Y, lax.rem(c, Y)
    zq = z // Q
    x, core = r // 2, lax.rem(r, 2)
    X = R // 2
    sens = NS // R
    part = sens // H
    npar = pbuf.shape[-1]
    partner = (r + 1 - 2 * core, c)

    lag_peer = lambda k: (lax.rem(r + k, R), c)
    x_peer = lambda k: (lax.rem(x + k, X) * 2 + core, c)
    y_peer = lambda k: (r, z * Y + lax.rem(y + k, Y))
    z_at = lambda t: (r, t * Y + y)
    z_peer = lambda k: z_at(lax.rem(z + k + Z, Z))

    def signal(sem, dev):
        pl.semaphore_signal(sem, inc=1, device_id=dev, device_id_type=MESH)

    def remote(src, dst, ssem, rsem, dev):
        return pltpu.make_async_remote_copy(
            src_ref=src, dst_ref=dst, send_sem=ssem, recv_sem=rsem, device_id=dev, device_id_type=MESH
        )

    sends = []

    def send(*a):
        cp = remote(*a)
        cp.start()
        sends.append(cp)
        return cp

    local = [
        pltpu.make_async_copy(probes_ref, pbuf.at[r], local_sem.at[0]),
        pltpu.make_async_copy(weight_hbm, weight_ref, local_sem.at[1]),
        pltpu.make_async_copy(mask_hbm, mask_ref, local_sem.at[2]),
    ]

    def lag_part(q, h):
        return lag_ref.at[:, pl.ds(pl.multiple_of(q * sens + h * part, part), part), :]

    for h in range(H):
        local.append(pltpu.make_async_copy(lag_part(r, h), lbuf.at[h, r], local_sem.at[3 + h]))
    for cp in local:
        cp.start()

    barrier = pltpu.get_barrier_semaphore()
    for k in range(1, R):
        signal(barrier, lag_peer(k))
    for k in range(1, Y):
        signal(barrier, y_peer(k))
    for k in (1, -1):
        signal(barrier, z_peer(k))
    pl.semaphore_wait(barrier, R + Y)

    def near_signal(i):
        for k in (1 << i, -(1 << i)):
            signal(near_sem.at[i], z_peer(k))

    def near_wait(i):
        pl.semaphore_wait(near_sem.at[i], 2)

    near_signal(0)

    pcps = [send(probes_ref, pbuf.at[r], ps_sem.at[0], pr_sem.at[0], partner)]
    for k in (2, 1, 3):
        pcps.append(send(probes_ref, pbuf.at[r], ps_sem.at[k], pr_sem.at[k], x_peer(k)))
    lcps = [[], []]
    for h in range(H):
        for k in (4, 5, 3, 2, 6, 7, 1):
            q = lax.rem(r + k, R)
            lcps[h].append(send(lag_part(q, h), lbuf.at[h, r], xs_sem.at[h, k], xr_sem.at[h, k], (q, c)))
    near_wait(0)
    near_signal(1)
    fcps = []
    for k in (1, 3, 2):
        pcps[{2: 1, 1: 2, 3: 3}[k]].wait_recv()
        src = lax.rem(x - k + X, X) * 2 + core
        fcps.append(send(pbuf.at[src], pbuf.at[src], fs_sem.at[k], fr_sem.at[k], partner))
    near_wait(1)
    near_signal(2)
    for cp in local:
        cp.wait()
    pcps[0].wait_recv()
    for cp in fcps:
        cp.wait_recv()

    rows = PROBES // Q

    def forward(h, start, count):
        acc = None
        for d in range(R):
            n = R - d
            lhs = jnp.concatenate(
                [pbuf[:n, b, pl.ds(start, count), :].reshape(n * count, npar) for b in range(J)], axis=1
            )
            term = lax.dot_general(
                lhs, toeplitz_block(lbuf.at[h], d), (((1,), (1,)), ((), ())), preferred_element_type=F32
            ).reshape(n, count, 128)
            if d == 0:
                acc = [term[a] for a in range(R)]
            else:
                for a in range(n):
                    acc[a + d] = acc[a + d] + term[a]
        for a in range(R):
            obs[h, a, pl.ds(start, count), :] = acc[a]

    def quarter(o):
        return lax.rem(zq + o, Q)

    def probes_of(q):
        return pl.ds(pl.multiple_of(q * rows, rows), rows)

    order = (2, 1, 3, 0)

    def sum_y_start(h, i):
        q = quarter(order[i])
        cps = []
        for k in range(1, Y):
            t = lax.rem(y + k, Y)
            cps.append(
                send(
                    obs.at[h, pl.ds(2 * t, 2), probes_of(q), :],
                    ry.at[h, i, k - 1], ys_sem.at[h, i, k], yr_sem.at[h, i, k], y_peer(k),
                )
            )
        return cps

    late = []

    def sum_z_start(h, i, ycps):
        o = order[i]
        q = quarter(o)
        total = obs[h, pl.ds(2 * y, 2), probes_of(q), :]
        for k in range(1, Y):
            ycps[k - 1].wait_recv()
            total = total + ry[h, i, k - 1]
        sz[h, i] = total
        for e in range(2):
            t = Q * q + 2 * e + h
            k = lax.rem(t - z + Z, Z)
            cp = remote(sz.at[h, i, e], rz.at[k], zs_sem.at[h, i, e], zr_sem.at[k], z_at(t))
            if o:
                cp.start()
                sends.append(cp)
            else:
                pl.when(t != z)(cp.start)
                late.append((t != z, cp))

    for cp in lcps[0]:
        cp.wait_recv()
    forward(0, 0, PROBES)
    ycps = [[sum_y_start(0, i) for i in range(Q)], []]
    for cp in lcps[1]:
        cp.wait_recv()
    for i in range(Q):
        forward(1, quarter(order[i]) * rows, rows)
        ycps[1].append(sum_y_start(1, i))
    near_wait(2)
    for h in range(H):
        for i in range(Q):
            sum_z_start(h, i, ycps[h][i])

    hz = lax.rem(z, H)

    def chip_row(v):
        out = v[0:1, :]
        for i in range(1, X):
            out = jnp.where(x == i, v[i : i + 1, :], out)
        return out

    row = chip_row(weight_ref[...])
    on = chip_row(mask_ref[...].astype(F32))
    own = sz[hz, 3, lax.rem(z, Q) // 2]
    for k in range(1, Z):
        remote(rz.at[k], rz.at[k], zs_sem.at[0, 0, 0], zr_sem.at[k], z_peer(k)).wait_recv()
        own = own + rz[k]
    both = row * on
    scale = jnp.zeros((1, 128), F32)
    for j in range(4):
        piece = both[:, j * part : (j + 1) * part]
        piece = jnp.concatenate([piece] * J, axis=1)
        scale = jnp.where(core * H + hz == j, piece, scale)
    wz[z] = (scale * own).astype(BF16)
    for k in (8, 7, 9, 6, 10, 5, 11, 4, 12, 3, 13, 2, 14, 1, 15):
        send(wz.at[z], wz.at[z], azs_sem.at[k], azr_sem.at[z], z_peer(k))
    arrive = (0, 1, 3, 2)
    aycps = []
    for i, o in enumerate(arrive):
        q = quarter(o)
        for e in range(Q):
            t = Q * q + e
            cp = remote(wz.at[t], wz.at[t], azs_sem.at[1], azr_sem.at[t], z_at(t))
            if o:
                cp.wait_recv()
            else:
                pl.when(t != z)(cp.wait_recv)
        aycps.append([])
        for k in range(1, Y):
            aycps[i].append(
                send(wz.at[pl.ds(Q * q, Q)], wy.at[q, y], ays_sem.at[i, k], ayr_sem.at[i, k], y_peer(k))
            )
        wy[q, y] = wz[pl.ds(Q * q, Q)]

    tot = [jnp.zeros((rows, 128), F32) for _ in range(H)]
    half = J * npar // 2

    def adjoint(i):
        q = quarter(arrive[i])
        for cp in aycps[i]:
            cp.wait_recv()
        w = []
        for a in range(R):
            e = 2 * (a % 2)
            w.append(jnp.concatenate([wy[q, a // 2, e], wy[q, a // 2, e + 1]], axis=1))
        for u in range(2):
            acc = None
            for d in range(R):
                n = R - d
                rhs = jnp.concatenate(
                    [toeplitz_block(lbuf.at[h], d)[:, u * half : (u + 1) * half] for h in range(H)], axis=0
                )
                term = jnp.dot(jnp.concatenate(w[d:], axis=0), rhs, preferred_element_type=F32)
                pieces = [term[a * rows : (a + 1) * rows] for a in range(n)]
                acc = pieces if d == 0 else [acc[a] + pieces[a] for a in range(n)] + acc[n:]
            for a in range(R):
                mis[i, a % 2, a // 2, :, u * half : (u + 1) * half] = acc[a]
        cps = []
        for k in (2, 1, 3, 0):
            t = lax.rem(x + k, X)
            cps.append(
                send(mis.at[i, 1 - core, t], md.at[i, k], ds_sem.at[i, k], dr_sem.at[i, k], partner)
            )
        for a in range(R):
            for h in range(H):
                v = w[a][:, 128 * h : 128 * h + 128].astype(F32)
                tot[h] = tot[h] + v * v
        return cps

    def sum_x_start(i, dcps):
        cps = []
        for n, k in enumerate((2, 1, 3)):
            t = lax.rem(x + k, X)
            dcps[n].wait_recv()
            send_x[i, k] = (mis[i, core, t] + md[i, k]).astype(BF16)
            cps.append(send(send_x.at[i, k], mx.at[i, k], ms_sem.at[i, k], mr_sem.at[i, k], x_peer(k)))
        return cps

    dcps, mcps = [], []
    for i in range(Q):
        dcps.append(adjoint(i))
        if i:
            mcps.append(sum_x_start(i - 1, dcps[i - 1]))

    def mine(v):
        return jnp.where(core == 0, v[:, :sens], v[:, sens:])

    sq = []
    for h in range(H):
        v = jnp.sum(tot[h], axis=0, keepdims=True)
        sq.append(sum(v[:, b * part : (b + 1) * part] for b in range(J)))
    sq = jnp.concatenate(sq, axis=1)
    wr = mine(row)
    g = mine(on) * sq / (wr * wr) * (1.0 / (R * J * PROBES))
    gsend[...] = jnp.broadcast_to(jnp.concatenate([g, g], axis=1), (8, 128))
    gcps = []
    for k in range(1, R):
        gcps.append(send(gsend, gbuf.at[r], gs_sem.at[k], gr_sem.at[k], lag_peer(k)))
    gbuf[r] = gsend[...]

    mcps.append(sum_x_start(Q - 1, dcps[Q - 1]))
    for i in range(Q):
        at = probes_of(quarter(arrive[i]))
        dcps[i][3].wait_recv()
        total = mis[i, core, x] + md[i, 0]
        total = total + jnp.concatenate([pbuf[r, b, at, :].astype(F32) for b in range(J)], axis=1)
        for n, k in ((1, 1), (2, 3), (0, 2)):
            mcps[i][n].wait_recv()
            total = total + mx[i, k].astype(F32)
        for b in range(J):
            out_ref[b, at, :] = total[:, b * npar : (b + 1) * npar]
    for cp in gcps:
        cp.wait_recv()
    grad_ref[...] = jnp.concatenate(
        [jnp.concatenate([gbuf[2 * q, 0:1, :sens], gbuf[2 * q + 1, 0:1, :sens]], axis=1) for q in range(X)], axis=0
    )
    for cp in sends:
        cp.wait_send()
    for cond, cp in late:
        pl.when(cond)(cp.wait_send)


def per_device(R, stop, probes, lag_blocks, sensor_weights, sensor_mask):
    npar = probes.shape[2]
    sens = NS // R
    part = sens // H
    X = R // 2
    dma = lambda *n: pltpu.SemaphoreType.DMA(n)
    out, grad = pl.pallas_call(
        functools.partial(kernel, R, stop),
        out_shape=(
            jax.ShapeDtypeStruct((J, PROBES, npar), F32),
            jax.ShapeDtypeStruct((NS // 128, 128), F32),
        ),
        in_specs=[pl.BlockSpec(memory_space=pltpu.HBM)] * 4,
        out_specs=(pl.BlockSpec(memory_space=pltpu.VMEM),) * 2,
        scratch_shapes=[
            pltpu.VMEM((R, J, PROBES, npar), BF16),
            pltpu.VMEM((H, R, J, part, npar), BF16),
            pltpu.VMEM((NS // 128, 128), F32),
            pltpu.VMEM((NS // 128, 128), jnp.int32),
            pltpu.VMEM((H, R, PROBES, 128), F32),
            pltpu.VMEM((H, Q, Y - 1, 2, PROBES // Q, 128), F32),
            pltpu.VMEM((H, Q, 2, PROBES // Q, 128), F32),
            pltpu.VMEM((Z, 16, 128), F32),
            pltpu.VMEM((Z, 16, 128), BF16),
            pltpu.VMEM((Q, Y, Q, 16, 128), BF16),
            pltpu.VMEM((Q, 2, X, PROBES // Q, J * npar), F32),
            pltpu.VMEM((Q, X, PROBES // Q, J * npar), F32),
            pltpu.VMEM((Q, X, PROBES // Q, J * npar), BF16),
            pltpu.VMEM((Q, X, PROBES // Q, J * npar), BF16),
            pltpu.VMEM((8, 128), F32),
            pltpu.VMEM((R, 8, 128), F32),
            pltpu.SemaphoreType.REGULAR((3,)),
            dma(5), dma(X), dma(X), dma(X), dma(X), dma(H, R), dma(H, R), dma(H, Q, Y), dma(H, Q, Y),
            dma(H, Q, 2), dma(Z), dma(Z), dma(Z), dma(Q, Y), dma(Q, Y), dma(Q, X), dma(Q, X), dma(Q, X), dma(Q, X),
            dma(R), dma(R),
        ],
        compiler_params=pltpu.CompilerParams(
            collective_id=0, has_side_effects=True, vmem_limit_bytes=48 * 1024 * 1024
        ),
        cost_estimate=pl.CostEstimate(flops=2 * 10**9, bytes_accessed=10**6, transcendentals=0),
        name="toeplitz",
    )(
        *(
            pltpu.with_memory_space_constraint(v, pltpu.HBM)
            for v in (probes, lag_blocks, sensor_weights.reshape(NS // 128, 128), sensor_mask.reshape(NS // 128, 128))
        )
    )
    return out, grad.reshape(NS)


def solution(mesh, stop=8):
    R = mesh.shape["lag"]
    return jax.shard_map(
        functools.partial(per_device, R, stop),
        mesh=mesh,
        in_specs=(P("lag", None, "par"), P("lag", None, "par"), P(), P()),
        out_specs=(P("lag", None, "par"), P()),
        check_vma=False,
    )
```
